256 devices in a mesh: qrow: 16 (over x, y_hi, core), ncol: 16 (over z, y_lo).
Axes of the slice: x: 4, y: 4 (y_hi: 2, y_lo: 2; y = y_hi * 2 + y_lo), z: 8, core: 2. Of those that a mesh axis runs over, the one named last changes fastest.
Arguments:
- query: bfloat16 [32768, 1024], P(('qrow', 'ncol')), may hold values from -6 to 6
- d_out: bfloat16 [32768, 1024], P(('qrow', 'ncol')), may hold values from -6 to 6
- out: bfloat16 [32768, 1024], P(('qrow', 'ncol')), may hold values from -6 to 6
- lse: float32 [8, 32768], P(None, ('qrow', 'ncol')), may hold values from 4.5 to 7.5
- keys: bfloat16 [8192, 1024], P(('ncol', 'qrow')), may hold values from -6 to 6
- values: bfloat16 [8192, 1024], P(('ncol', 'qrow')), may hold values from -6 to 6
- tile_blocks: int32 [16, 16, 2, 32], P('qrow', 'ncol'), may hold values from 0 to 15, as said below
- tile_count: int32 [16, 16], P('qrow', 'ncol'), may hold values from 1 to 32, as said below
Outputs:
- d_query: bfloat16 [32768, 1024], P(('qrow', 'ncol'))
- d_keys: bfloat16 [8192, 1024], P(('ncol', 'qrow'))
- d_values: bfloat16 [8192, 1024], P(('ncol', 'qrow'))
The draws below stay inside these ranges and needn't reach their ends.
Inputs may be any that keep to these rules, and one draw needn't show every extreme that they name: `tile_blocks`: in cell (r, c), slots t < tile_count[r, c] name distinct pairs: entry 0 a query block below 16, entry 1 a node block below 4; later slots hold 0. `tile_count`: some cell lists exactly 32 tiles.
All inputs are finite; a program needn't handle non-finite values.
Results may differ from the reference program's by a relative error of at most 0.0051.
Values may be sent and summed in bfloat16 or wider, within the bound.
No kernel may reach another device: no remote copies, remote signals or barrier semaphores. Data moves between devices by JAX's collectives and lax.ppermute only.
A program may use at most 128 MiB of HBM per device.

```python
import jax
import jax.numpy as jnp
from jax import lax

H = 8
HD = 128
BLOCK = 128
QB_ROW = 16
NODE_BLOCKS_PER = 4
TILES_DEV = 32
D = 1024
QTOK = 32768
NTOK = 8192
N_QROW = 16
N_NCOL = 16


def plan_tiles(key):
    row_total = N_QROW
    col_total = N_NCOL
    pairing_count = QB_ROW * NODE_BLOCKS_PER
    split_keys = jax.random.split(key, 6)
    row_order = jax.random.permutation(split_keys[0], row_total)
    hub_rows = jnp.zeros((row_total,), jnp.int32).at[row_order[:min(2, row_total)]].set(1)
    quarter = TILES_DEV // 4
    hub_totals = TILES_DEV - jax.random.randint(split_keys[1], (row_total, col_total), 0, quarter + 1)
    drawn_totals = jax.random.randint(split_keys[2], (row_total, col_total), quarter, TILES_DEV * 5 // 8 + 1)
    totals = jnp.where(hub_rows[:, None] == 1, hub_totals, drawn_totals)
    totals = jnp.maximum(totals, 1)
    chosen_col = jax.random.randint(split_keys[3], (), 0, col_total)
    row_grid = jnp.arange(row_total)[:, None]
    col_grid = jnp.arange(col_total)[None, :]
    totals = jnp.where((row_grid == row_order[0]) & (col_grid == chosen_col), TILES_DEV, totals).astype(jnp.int32)
    central_block = jax.random.randint(split_keys[4], (row_total, 1, 1), 0, QB_ROW)
    pairing_index = jnp.arange(pairing_count, dtype=jnp.int32)
    extra_credit = jnp.where(pairing_index[None, None, :] // NODE_BLOCKS_PER == central_block, 65536, 0).astype(jnp.int32)
    random_jitter = jax.random.randint(split_keys[5], (row_total, col_total, pairing_count), 0, 65536).astype(jnp.int32)
    ranking_weight = (random_jitter + extra_credit) * pairing_count + pairing_index[None, None, :]
    picked = jnp.argsort(-ranking_weight, axis=-1, stable=True)[:, :, :TILES_DEV].astype(jnp.int32)
    slot_alive = jnp.arange(TILES_DEV)[None, None, :] < totals[:, :, None]
    query_part = jnp.where(slot_alive, picked // NODE_BLOCKS_PER, 0)
    node_part = jnp.where(slot_alive, picked % NODE_BLOCKS_PER, 0)
    blocks = jnp.stack([query_part, node_part], axis=2).astype(jnp.int32)
    return (blocks, totals)


def draw_tile_blocks(key, part):
    blocks, totals = plan_tiles(key)
    return blocks


def draw_tile_count(key, part):
    blocks, totals = plan_tiles(key)
    return totals


def block_scale(key, extent, shards, smallest, high):
    level, own = 1.0, jax.random.fold_in(key, 6)
    for axis_at, blocks in shards:
        draws = jnp.exp(jax.random.uniform(jax.random.fold_in(own, axis_at), (blocks,), jnp.float32, smallest / len(shards), high / len(shards)))
        level = level * jnp.repeat(draws, extent[axis_at] // blocks).reshape([-1 if axis == axis_at else 1 for axis in range(len(extent))])
    return level


def bell_draw(own_key, extent, spread, limit, pieces=(), kind=jnp.bfloat16):
    gain = block_scale(own_key, extent, pieces, -0.22, 0.18) if pieces else 1.0
    array = jax.random.normal(own_key, extent, jnp.float32) * spread * gain
    return jnp.minimum(jnp.maximum(array, -limit), limit).astype(kind)


def setup_inputs(seed: int = 0) -> dict:
    arg_keys = jax.random.split(jax.random.key(seed), 9)
    return {
        "query": bell_draw(arg_keys[0], (QTOK, D), 1.0, 6.0, ((0, 256),)),
        "d_out": bell_draw(arg_keys[1], (QTOK, D), 1.0, 6.0, ((0, 256),)),
        "out": bell_draw(arg_keys[2], (QTOK, D), 1.0, 6.0, ((0, 256),)),
        "lse": jnp.clip(4.5 + 3.0 * jax.random.uniform(arg_keys[3], (H, QTOK), jnp.float32) ** block_scale(arg_keys[3], (H, QTOK), ((1, 256),), -0.2, 0.2), 4.5, 7.5),
        "keys": bell_draw(arg_keys[4], (NTOK, D), 1.0, 6.0, ((0, 256),)),
        "values": bell_draw(arg_keys[5], (NTOK, D), 1.0, 6.0, ((0, 256),)),
        "tile_blocks": draw_tile_blocks(jax.random.fold_in(arg_keys[8], 71), 0),
        "tile_count": draw_tile_count(jax.random.fold_in(arg_keys[8], 71), 0),
    }


def reference(query, d_out, out, lse, keys, values, tile_blocks, tile_count):
    softmax_scale = HD ** -0.5
    model_width = H * HD
    highest = lax.Precision.HIGHEST
    product_rows = d_out.astype(jnp.float32) * out.astype(jnp.float32)
    row_delta = jnp.sum(product_rows.reshape(QTOK, H, HD), axis=2)
    query_index = (jnp.arange(N_QROW, dtype=jnp.int32)[:, None, None] * QB_ROW + tile_blocks[:, :, 0, :]).reshape(-1).astype(jnp.int32)
    node_index = (jnp.arange(N_NCOL, dtype=jnp.int32)[None, :, None] * NODE_BLOCKS_PER + tile_blocks[:, :, 1, :]).reshape(-1).astype(jnp.int32)
    slot_alive = (jnp.arange(TILES_DEV, dtype=jnp.int32)[None, None, :] < tile_count[:, :, None]).reshape(-1)

    def work(grads, query_block, node_block):
        grad_query, grad_keys, grad_values = grads
        query_start = (query_block * BLOCK).astype(jnp.int32)
        node_start = (node_block * BLOCK).astype(jnp.int32)
        query_tile = lax.dynamic_slice_in_dim(query, query_start, BLOCK, 0).astype(jnp.float32).reshape(BLOCK, H, HD)
        grad_tile = lax.dynamic_slice_in_dim(d_out, query_start, BLOCK, 0).astype(jnp.float32).reshape(BLOCK, H, HD)
        key_tile = lax.dynamic_slice_in_dim(keys, node_start, BLOCK, 0).astype(jnp.float32).reshape(BLOCK, H, HD)
        value_tile = lax.dynamic_slice_in_dim(values, node_start, BLOCK, 0).astype(jnp.float32).reshape(BLOCK, H, HD)
        lse_tile = lax.dynamic_slice_in_dim(lse, query_start, BLOCK, 1)
        delta_tile = lax.dynamic_slice_in_dim(row_delta, query_start, BLOCK, 0).T
        scores = jnp.einsum('qhd,khd->hqk', query_tile, key_tile, precision=highest) * softmax_scale
        weights = jnp.exp(scores - lse_tile[:, :, None])
        grad_weights = jnp.einsum('qhd,khd->hqk', grad_tile, value_tile, precision=highest)
        grad_scores = weights * (grad_weights - delta_tile[:, :, None])
        weights_low = lax.optimization_barrier(weights.astype(jnp.bfloat16)).astype(jnp.float32)
        scores_low = lax.optimization_barrier(grad_scores.astype(jnp.bfloat16)).astype(jnp.float32)
        value_part = jnp.einsum('hqk,qhd->khd', weights_low, grad_tile, precision=highest).reshape(BLOCK, model_width)
        key_part = jnp.einsum('hqk,qhd->khd', scores_low, query_tile, precision=highest).reshape(BLOCK, model_width) * softmax_scale
        query_part = jnp.einsum('hqk,khd->qhd', scores_low, key_tile, precision=highest).reshape(BLOCK, model_width) * softmax_scale
        old_query = lax.dynamic_slice_in_dim(grad_query, query_start, BLOCK, 0)
        old_keys = lax.dynamic_slice_in_dim(grad_keys, node_start, BLOCK, 0)
        old_values = lax.dynamic_slice_in_dim(grad_values, node_start, BLOCK, 0)
        grad_query = lax.dynamic_update_slice_in_dim(grad_query, old_query + query_part, query_start, 0)
        grad_keys = lax.dynamic_update_slice_in_dim(grad_keys, old_keys + key_part, node_start, 0)
        grad_values = lax.dynamic_update_slice_in_dim(grad_values, old_values + value_part, node_start, 0)
        return (grad_query, grad_keys, grad_values)

    def visit(grads, item):
        query_block, node_block, alive = item
        grads = lax.cond(alive, lambda held: work(held, query_block, node_block), lambda held: held, grads)
        return grads, None

    start_grads = (jnp.zeros((QTOK, model_width), jnp.float32), jnp.zeros((NTOK, model_width), jnp.float32), jnp.zeros((NTOK, model_width), jnp.float32))
    final_grads, unused = lax.scan(visit, start_grads, (query_index, node_index, slot_alive))
    grad_query, grad_keys, grad_values = final_grads
    return (grad_query.astype(jnp.bfloat16), grad_keys.astype(jnp.bfloat16), grad_values.astype(jnp.bfloat16))
```

```python
import functools

import jax
import jax.numpy as jnp
from jax import lax
from jax.experimental import pallas as pl
from jax.experimental.pallas import tpu as pltpu
from jax.sharding import PartitionSpec as P


BLOCK = 128
HEADS = 8
HD = 128
D = 1024
SHARD = 32
AUX = 16
PACKED = 2 * BLOCK + AUX
AXES = ("qrow", "ncol")
SCALE = HD ** (-0.5)
LOG2E = 1.4426950408889634


def device_index(x, yh, core, z, yl):
    return (x * 4 + yh * 2 + core) * 16 + z * 2 + yl


def make_perm(target):
    pairs = []
    for x in range(4):
        for yh in range(2):
            for core in range(2):
                for z in range(8):
                    for yl in range(2):
                        pairs.append(
                            (
                                device_index(x, yh, core, z, yl),
                                device_index(*target(x, yh, core, z, yl)),
                            )
                        )
    return pairs


def y_step(d):
    def target(x, yh, core, z, yl):
        y = (yh * 2 + yl + d) % 4
        return (x, y // 2, core, z, y % 2)

    return make_perm(target)


def x_step(d):
    return make_perm(lambda x, yh, core, z, yl: ((x + d) % 4, yh, core, z, yl))


def z_step(d):
    return make_perm(lambda x, yh, core, z, yl: (x, yh, core, (z + d) % 8, yl))


def z_home(d):
    return make_perm(lambda x, yh, core, z, yl: (x, yh, yl, (z + d) % 8, core))


CORE = make_perm(lambda x, yh, core, z, yl: (x, yh, 1 - core, z, yl))
OTHER_CELL = make_perm(lambda x, yh, core, z, yl: (x, yh, 1 - yl, z, core))


def send(array, perm):
    return lax.ppermute(array, AXES, perm)


def split3(value):
    high = value.astype(jnp.bfloat16).astype(jnp.float32)
    rest = value - high
    middle = rest.astype(jnp.bfloat16).astype(jnp.float32)
    return high, middle, rest - middle


def pack_kernel(grad_ref, out_ref, lse_ref, packed_ref):
    packed_ref[pl.ds(0, BLOCK), :] = grad_ref[...]
    row = lax.broadcasted_iota(jnp.int32, (AUX, BLOCK), 0)
    for h in range(HEADS):
        cols = pl.ds(h * HD, HD)
        product = grad_ref[:, cols].astype(jnp.float32) * out_ref[:, cols].astype(jnp.float32)
        delta = jnp.sum(product.T, axis=0, keepdims=True)
        parts = split3(lse_ref[pl.ds(h, 1), :]) + split3(delta)
        aux = jnp.zeros((AUX, BLOCK), jnp.float32)
        for at, part in enumerate(parts):
            aux = jnp.where(row == at, jnp.broadcast_to(part, (AUX, BLOCK)), aux)
        packed_ref[pl.ds(BLOCK, AUX), cols] = aux.astype(jnp.bfloat16)


def pack(d_out, out, lse):
    return pl.pallas_call(
        pack_kernel,
        out_shape=jax.ShapeDtypeStruct((BLOCK + AUX, D), jnp.bfloat16),
        compiler_params=pltpu.CompilerParams(vmem_limit_bytes=16 * 2**20),
        cost_estimate=pl.CostEstimate(flops=2 * BLOCK * D, bytes_accessed=800_000, transcendentals=0),
    )(d_out, out, lse)


def tile_kernel(n, mask_ref, *refs):
    refs = list(refs)

    def take(count):
        got = refs[:count]
        del refs[:count]
        return got

    q_in, g_in = take(n), take(n)
    nodes_in = take(6)
    outs = take(4)
    dq_out = take(n + 1)
    kbuf, vbuf, kturn, qbuf, wide_in, wide_out, dkv, dq, listed, sems = take(10)
    count = [0]

    def start(src, dst):
        copy = pltpu.make_async_copy(src, dst, sems.at[count[0]])
        count[0] += 1
        copy.start()
        return copy

    copies = []
    for dx in range(4):
        for core in range(2):
            piece = nodes_in[4 + dx // 2].at[pl.ds(dx % 2 * 256, 256)] if core else nodes_in[dx]
            for dy in range(4):
                rows = pl.ds((dx * 2 + dy % 2) * BLOCK + (core * 2 + dy // 2) * SHARD, SHARD)
                copies.append(start(piece.at[pl.ds(dy * 64, SHARD)], kbuf.at[rows]))
                copies.append(start(piece.at[pl.ds(dy * 64 + SHARD, SHARD)], vbuf.at[rows]))
    for i in range(n):
        copies.append(start(q_in[i], qbuf.at[pl.ds(i * PACKED, BLOCK)]))
        copies.append(start(g_in[i], qbuf.at[pl.ds(i * PACKED + BLOCK, BLOCK + AUX)]))
    dq[...] = jnp.zeros_like(dq)
    wide_in[...] = jnp.zeros_like(wide_in)
    wide_out[...] = jnp.zeros_like(wide_out)
    dkv[...] = jnp.zeros_like(dkv)
    for copy in copies:
        copy.wait()
    for h in range(HEADS):
        for j in range(8):
            block = kbuf[pl.ds(j * BLOCK, BLOCK), pl.ds(h * HD, HD)]
            kturn[j, pl.ds(h * HD, HD), :] = block.T

    def pair(i, ja, jb, dead):
        rows_a = pl.ds(pl.multiple_of(ja * BLOCK, BLOCK), BLOCK)
        rows_b = pl.ds(pl.multiple_of(jb * BLOCK, BLOCK), BLOCK)
        aux_rows = pl.ds(pl.multiple_of(i * PACKED + 2 * BLOCK, AUX), AUX)
        second = lax.broadcasted_iota(jnp.int32, (2 * BLOCK, 1), 0) >= BLOCK
        shut = jnp.where(second, dead, 0.0)

        def first_dot(h):
            cols = pl.ds(h * HD, HD)
            k = jnp.concatenate([kbuf[rows_a, cols], kbuf[rows_b, cols]], axis=0)
            v = jnp.concatenate([vbuf[rows_a, cols], vbuf[rows_b, cols]], axis=0)
            return jnp.dot(
                jnp.concatenate([k, v], axis=1), wide_in[h], preferred_element_type=jnp.float32
            )

        def middle(h, both):
            cols = pl.ds(h * HD, HD)
            aux = qbuf[aux_rows, cols].astype(jnp.float32)
            lse = (aux[0:1] + aux[1:2] + aux[2:3]) * LOG2E
            delta = aux[3:4] + aux[4:5] + aux[5:6]
            weights = jnp.exp2(both[:, :HD] * (SCALE * LOG2E) - (lse + shut))
            scores_low = (weights * (both[:, HD:] - delta)).astype(jnp.bfloat16)
            return weights.astype(jnp.bfloat16), scores_low

        def node_dot(h, lows):
            wide = pl.ds(h * 2 * HD, 2 * HD)
            part = jnp.dot(
                jnp.concatenate(lows, axis=1), wide_out[h], preferred_element_type=jnp.float32
            )
            dkv[rows_a, wide] += part[:BLOCK]
            dkv[rows_b, wide] += part[BLOCK:]

        def query_dot(h, low):
            cols = pl.ds(h * HD, HD)
            k_turned = jnp.concatenate([kturn[ja, cols, :], kturn[jb, cols, :]], axis=1)
            dq[pl.ds(pl.multiple_of(i * D, D) + h * HD, HD), :] += jnp.dot(
                k_turned, low, preferred_element_type=jnp.float32
            )

        def query_dots(h, even_low, low):
            two = pl.ds(h * HD, 2 * HD)
            turned = jnp.dot(
                jnp.concatenate([kturn[ja, two, :], kturn[jb, two, :]], axis=1),
                jnp.concatenate([even_low, low], axis=1),
                preferred_element_type=jnp.float32,
            )
            at = pl.multiple_of(i * D, D) + h * HD
            dq[pl.ds(at, HD), :] += turned[:HD, :HD]
            dq[pl.ds(at + HD, HD), :] += turned[HD:, HD:]


        lows = [middle(h, first_dot(h)) for h in range(HEADS)]
        for h in range(HEADS):
            node_dot(h, lows[h])
        for h in range(0, HEADS, 2):
            query_dots(h, lows[h][1], lows[h + 1][1])

    @pl.loop(0, n)
    def _(i):
        total = jnp.int32(0)
        last_one = jnp.int32(0)
        for j in range(8):
            here = mask_ref[i * 8 + j]
            listed[total] = j
            last_one = jnp.where(here != 0, j, last_one)
            total = total + here
        listed[total] = last_one

        @pl.when(total > 0)
        def _():
            rows = pl.ds(pl.multiple_of(i * PACKED, AUX), BLOCK)
            grad_rows = pl.ds(pl.multiple_of(i * PACKED + BLOCK, AUX), BLOCK)
            for h in range(HEADS):
                cols = pl.ds(h * HD, HD)
                q, g = qbuf[rows, cols], qbuf[grad_rows, cols]
                wide_in[h, pl.ds(0, HD), pl.ds(0, HD)] = q.T
                wide_in[h, pl.ds(HD, HD), pl.ds(HD, HD)] = g.T
                wide_out[h, pl.ds(0, HD), pl.ds(0, HD)] = g
                wide_out[h, pl.ds(HD, HD), pl.ds(HD, HD)] = q

            @pl.loop(0, (total + 1) // 2)
            def _(p):
                alone = 2 * p + 1 >= total
                dead = jnp.where(alone, jnp.float32(1e30), jnp.float32(0.0))
                pair(i, listed[2 * p], listed[2 * p + 1], dead)

    for i in range(n):
        for h in range(HEADS):
            cols = pl.ds(h * HD, HD)
            turned = (dq[pl.ds(i * D + h * HD, HD), :] * SCALE).astype(jnp.bfloat16).T
            if i == n - 1:
                dq_out[i][:, cols] = turned[:64]
                dq_out[i + 1][:, cols] = turned[64:]
            else:
                dq_out[i][:, cols] = turned
    for core in range(2):
        for dx in range(4):
            for dy in range(4):
                rows = pl.ds((dx * 2 + dy % 2) * BLOCK + (core * 2 + dy // 2) * SHARD, SHARD)
                k_to = pl.ds((dx * 4 + dy) * SHARD, SHARD)
                v_to = pl.ds((dy * 4 + dx) * SHARD, SHARD)
                for h in range(HEADS):
                    cols = pl.ds(h * HD, HD)
                    part = dkv[rows, pl.ds(h * 2 * HD, HD)]
                    outs[2 + core][v_to, cols] = part.astype(jnp.bfloat16)
                    part = dkv[rows, pl.ds(h * 2 * HD + HD, HD)] * SCALE
                    outs[core][k_to, cols] = part.astype(jnp.bfloat16)


def tiles(mask, q_blocks, g_blocks, nodes):
    n = len(q_blocks)
    bf16, f32 = jnp.bfloat16, jnp.float32
    scratch = [
        pltpu.VMEM((1024, D), bf16),
        pltpu.VMEM((1024, D), bf16),
        pltpu.VMEM((8, 1024, BLOCK), bf16),
        pltpu.VMEM((n * PACKED, D), bf16),
        pltpu.VMEM((HEADS, 2 * HD, 2 * HD), bf16),
        pltpu.VMEM((HEADS, 2 * HD, 2 * HD), bf16),
        pltpu.VMEM((1024, 2 * D), f32),
        pltpu.VMEM((n * D, BLOCK), f32),
        pltpu.SMEM((16,), jnp.int32),
        pltpu.SemaphoreType.DMA((64 + 2 * n,)),
    ]
    sums = [jax.ShapeDtypeStruct((512, D), bf16)] * 4
    blocks = [jax.ShapeDtypeStruct((BLOCK, D), bf16)] * (n - 1)
    blocks += [jax.ShapeDtypeStruct((64, D), bf16)] * 2
    args = list(q_blocks) + list(g_blocks) + list(nodes)
    out = pl.pallas_call(
        functools.partial(tile_kernel, n),
        out_shape=sums + blocks,
        in_specs=[pl.BlockSpec(memory_space=pltpu.SMEM)]
        + [pl.BlockSpec(memory_space=pltpu.HBM)] * len(args),
        out_specs=[pl.BlockSpec(memory_space=pltpu.VMEM)] * (len(sums) + len(blocks)),
        scratch_shapes=scratch,
        compiler_params=pltpu.CompilerParams(vmem_limit_bytes=40 * 2**20),
        cost_estimate=pl.CostEstimate(
            flops=20_000_000_000, bytes_accessed=12_000_000, transcendentals=0
        ),
    )(mask, *args)
    return list(out[:4]), list(out[4:])


def fence_kernel(*refs):
    pass


def fence(*arrays, space=pltpu.HBM):
    any_space = pl.BlockSpec(memory_space=space)
    return pl.pallas_call(
        fence_kernel,
        out_shape=[jax.ShapeDtypeStruct(a.shape, a.dtype) for a in arrays],
        in_specs=[any_space] * len(arrays),
        out_specs=[any_space] * len(arrays),
        input_output_aliases={at: at for at in range(len(arrays))},
        compiler_params=pltpu.CompilerParams(vmem_limit_bytes=2**20),
        cost_estimate=pl.CostEstimate(flops=10_000_000_000, bytes_accessed=4096, transcendentals=0),
    )(*arrays)


def plain_call(kernel, out_shapes, *arrays):
    return pl.pallas_call(
        kernel,
        out_shape=[jax.ShapeDtypeStruct(shape, jnp.bfloat16) for shape in out_shapes],
        compiler_params=pltpu.CompilerParams(vmem_limit_bytes=16 * 2**20),
        cost_estimate=pl.CostEstimate(flops=5_000_000_000, bytes_accessed=4_000_000, transcendentals=0),
    )(*arrays)


def wide_sum(*parts):
    total = parts[0].astype(jnp.float32)
    for part in parts[1:]:
        total = total + part.astype(jnp.float32)
    return total.astype(jnp.bfloat16)


def sum_kernel_1(far_a, far_b, up, down, k_own, k_got, v_own, v_got, up_out, down_out, *pieces):
    low, high = pl.ds(0, 64), pl.ds(64, 64)
    up_out[low, :] = wide_sum(far_a[...], up[low, :])
    up_out[high, :] = up[high, :]
    down_out[low, :] = down[low, :]
    down_out[high, :] = wide_sum(far_b[...], down[high, :])
    for d in range(4):
        rows = pl.ds(d * BLOCK, BLOCK)
        pieces[d][...] = wide_sum(k_own[rows, :], k_got[rows, :])
        pieces[4 + d][...] = wide_sum(v_own[rows, :], v_got[rows, :])


def hop_kernel(up_got, up, down_got, down, token, up_out, down_out, token_out):
    up_out[...] = wide_sum(up_got[...], up[...])
    down_out[...] = wide_sum(down_got[...], down[...])
    token_out[...] = token[...]


def node_kernel_1(*refs):
    k_parts, v_parts, outs = refs[:4], refs[4:8], refs[9:]
    for d in range(4):
        rows = pl.ds(d * SHARD, SHARD)
        outs[d][...] = wide_sum(*[part[rows, :] for part in k_parts])
        outs[4 + d][...] = wide_sum(*[part[rows, :] for part in v_parts])


def node_kernel_2(*refs):
    refs[8][...] = wide_sum(*[part[...] for part in refs[:4]])
    refs[9][...] = wide_sum(*[part[...] for part in refs[4:8]])


def home_kernel(own, up_got, down_got, token, out, token_out):
    out[...] = wide_sum(own[...], up_got[...], down_got[...])
    token_out[...] = token[...]


def local(query, d_out, out, lse, keys, values, tile_blocks, tile_count):
    row, col = lax.axis_index("qrow"), lax.axis_index("ncol")
    x, core, z, yl = row // 4, row % 2, col // 2, col % 2
    home = z_home(0)
    up, down = z_step(1), z_step(-1)
    whole, shard = (BLOCK, D), (SHARD, D)

    token = jnp.zeros((8, 128), jnp.float32)
    cell = jnp.concatenate(
        [tile_blocks.reshape(64), tile_count.reshape(1), jnp.zeros((63,), jnp.int32)]
    ).reshape(1, 128)
    q, g = {0: send(query, home)}, {}
    group = (0, 1, -1, 2, -2, 3, -3, 4)
    kv = jnp.concatenate([keys, values], axis=0)
    kv_y = [kv] + [send(kv, y_step(-d)) for d in (1, 3, 2)]
    g[0] = send(pack(d_out, out, lse), home)
    token, q[0] = fence(token, q[0])
    q[-1], q[1] = send(q[0], up), send(q[0], down)
    kv_y = jnp.concatenate([kv_y[0], kv_y[1], kv_y[3], kv_y[2]], axis=0)
    token, g[0], kv_y = fence(token, g[0], kv_y)
    kv_x = {1: send(kv_y, x_step(-1))}
    g[-1], g[1] = send(g[0], up), send(g[0], down)
    token, q[-1], q[1] = fence(token, q[-1], q[1])
    q[-2], q[2] = send(q[-1], up), send(q[1], down)
    token, g[-1], g[1], kv_x[1], kv_y = fence(token, g[-1], g[1], kv_x[1], kv_y)
    g[-2], g[2] = send(g[-1], up), send(g[1], down)
    kv_x[3] = send(kv_y, x_step(-3))
    token, q[-2], q[2] = fence(token, q[-2], q[2])
    q[-3], q[3] = send(q[-2], up), send(q[2], down)
    token, g[-2], g[2], kv_x[3], kv_y = fence(token, g[-2], g[2], kv_x[3], kv_y)
    g[-3], g[3] = send(g[-2], up), send(g[2], down)
    kv_x[2] = send(kv_y, x_step(-2))
    kv_x[0] = kv_y
    cells = [(send(cell, home), core), (send(cell, OTHER_CELL), 1 - core)]
    mask = jnp.zeros((64,), jnp.bool_)
    for got, column in cells:
        a, b, count = got[0, 0:32], got[0, 32:64], got[0, 64]
        alive = (jnp.arange(32) < count) & ((a & 1) == core)
        slot = (((a >> 1) - z) & 7) * 8 + ((b - x) & 3) * 2 + (column ^ yl)
        hits = alive[:, None] & (slot[:, None] == jnp.arange(64)[None, :])
        mask = mask | jnp.any(hits, axis=0)
    mask = mask.astype(jnp.int32).reshape(8, 8)[jnp.array([o % 8 for o in group])].reshape(64)

    token, q[-3], q[3] = fence(token, q[-3], q[3])
    q[4] = send(q[-3], up)
    low_pieces = jnp.concatenate([kv_x[0], kv_x[1]], axis=0)
    token, g[-3], g[3], q[4], kv_x[2], low_pieces, mask = fence(
        token, g[-3], g[3], q[4], kv_x[2], low_pieces, mask
    )
    g[4] = send(g[3], down)
    low_got = send(low_pieces, CORE)
    high_got = send(jnp.concatenate([kv_x[2], kv_x[3]], axis=0), CORE)
    nodes = [kv_x[0], kv_x[1], kv_x[2], kv_x[3], low_got, high_got]

    sums, parts = tiles(mask, [q[o] for o in group], [g[o] for o in group], nodes)
    dq = dict(zip(group, parts))
    k_own, k_oth, v_own, v_oth = sums

    k_got, v_got = send(k_oth, CORE), send(v_oth, CORE)
    own = send(dq[0], home)
    held = plain_call(
        sum_kernel_1, [whole] * 10,
        send(parts[7], up), send(parts[8], down), dq[3], dq[-3], k_own, k_got, v_own, v_got,
    )
    up_low, down_low = held[0], held[1]
    k_low, v_low = list(held[2:6]), list(held[6:10])
    k_parts, v_parts = [k_low[0]] + [None] * 3, [v_low[0]] + [None] * 3
    k_parts[1], k_parts[3] = send(k_low[1], x_step(1)), send(k_low[3], x_step(3))
    v_parts[1] = send(v_low[1], y_step(1))
    token = jnp.zeros((16, 128), jnp.bfloat16)
    hop_shapes = [whole, whole, token.shape]
    up_low, down_low, token = plain_call(
        hop_kernel, hop_shapes, send(up_low, up), dq[2], send(down_low, down), dq[-2], token
    )
    up_got, down_got = send(up_low, up), send(down_low, down)
    token, own, k_parts[1], k_parts[3], v_parts[1], k_low[2], v_low[2], v_low[3] = fence(
        token, own, k_parts[1], k_parts[3], v_parts[1], k_low[2], v_low[2], v_low[3],
        space=pl.ANY,
    )
    k_parts[2] = send(k_low[2], x_step(2))
    v_parts[3], v_parts[2] = send(v_low[3], y_step(3)), send(v_low[2], y_step(2))
    up_low, down_low, token = plain_call(
        hop_kernel, hop_shapes, up_got, dq[1], down_got, dq[-1], token
    )
    up_got, down_got = send(up_low, z_home(1)), send(down_low, z_home(-1))
    grad_query, token = plain_call(home_kernel, [whole, token.shape], own, up_got, down_got, token)
    held = plain_call(node_kernel_1, [shard] * 8, *k_parts, *v_parts, token)
    k_parts = [held[0]] + [send(held[d], y_step(d)) for d in (1, 2, 3)]
    v_parts = [held[4]] + [send(held[4 + d], x_step(d)) for d in (1, 2, 3)]
    grad_keys, grad_values = plain_call(node_kernel_2, [shard] * 2, *k_parts, *v_parts)
    return grad_query, grad_keys, grad_values


def solution(mesh):
    in_specs = (
        P(("qrow", "ncol"), None),
        P(("qrow", "ncol"), None),
        P(("qrow", "ncol"), None),
        P(None, ("qrow", "ncol")),
        P(("ncol", "qrow"), None),
        P(("ncol", "qrow"), None),
        P("qrow", "ncol", None, None),
        P("qrow", "ncol"),
    )
    out_specs = (P(("qrow", "ncol"), None), P(("ncol", "qrow"), None), P(("ncol", "qrow"), None))
    return jax.shard_map(local, mesh=mesh, in_specs=in_specs, out_specs=out_specs, check_vma=False)
```

```python
import functools

import jax
import jax.numpy as jnp
from jax import lax
from jax.experimental import pallas as pl
from jax.experimental.pallas import tpu as pltpu
from jax.sharding import PartitionSpec as P


BLOCK = 128
HEADS = 8
HD = 128
D = 1024
SHARD = 32
AUX = 16
PACKED = 2 * BLOCK + AUX
AXES = ("qrow", "ncol")
SCALE = HD ** (-0.5)
LOG2E = 1.4426950408889634


def device_index(x, yh, core, z, yl):
    return (x * 4 + yh * 2 + core) * 16 + z * 2 + yl


def make_perm(target):
    pairs = []
    for x in range(4):
        for yh in range(2):
            for core in range(2):
                for z in range(8):
                    for yl in range(2):
                        pairs.append(
                            (
                                device_index(x, yh, core, z, yl),
                                device_index(*target(x, yh, core, z, yl)),
                            )
                        )
    return pairs


def y_step(d):
    def target(x, yh, core, z, yl):
        y = (yh * 2 + yl + d) % 4
        return (x, y // 2, core, z, y % 2)

    return make_perm(target)


def x_step(d):
    return make_perm(lambda x, yh, core, z, yl: ((x + d) % 4, yh, core, z, yl))


def z_step(d):
    return make_perm(lambda x, yh, core, z, yl: (x, yh, core, (z + d) % 8, yl))


def z_home(d):
    return make_perm(lambda x, yh, core, z, yl: (x, yh, yl, (z + d) % 8, core))


CORE = make_perm(lambda x, yh, core, z, yl: (x, yh, 1 - core, z, yl))
OTHER_CELL = make_perm(lambda x, yh, core, z, yl: (x, yh, 1 - yl, z, core))


def send(array, perm):
    return lax.ppermute(array, AXES, perm)


def split3(value):
    high = value.astype(jnp.bfloat16).astype(jnp.float32)
    rest = value - high
    middle = rest.astype(jnp.bfloat16).astype(jnp.float32)
    return high, middle, rest - middle


def pack_kernel(grad_ref, out_ref, lse_ref, packed_ref):
    packed_ref[pl.ds(0, BLOCK), :] = grad_ref[...]
    row = lax.broadcasted_iota(jnp.int32, (AUX, BLOCK), 0)
    for h in range(HEADS):
        cols = pl.ds(h * HD, HD)
        product = grad_ref[:, cols].astype(jnp.float32) * out_ref[:, cols].astype(jnp.float32)
        delta = jnp.sum(product.T, axis=0, keepdims=True)
        parts = split3(lse_ref[pl.ds(h, 1), :]) + split3(delta)
        aux = jnp.zeros((AUX, BLOCK), jnp.float32)
        for at, part in enumerate(parts):
            aux = jnp.where(row == at, jnp.broadcast_to(part, (AUX, BLOCK)), aux)
        packed_ref[pl.ds(BLOCK, AUX), cols] = aux.astype(jnp.bfloat16)


def pack(d_out, out, lse):
    return pl.pallas_call(
        pack_kernel,
        out_shape=jax.ShapeDtypeStruct((BLOCK + AUX, D), jnp.bfloat16),
        compiler_params=pltpu.CompilerParams(vmem_limit_bytes=16 * 2**20),
        cost_estimate=pl.CostEstimate(flops=20_000_000_000, bytes_accessed=800_000, transcendentals=0),
    )(d_out, out, lse)


def tile_kernel(n, mask_ref, *refs):
    refs = list(refs)

    def take(count):
        got = refs[:count]
        del refs[:count]
        return got

    q_in, g_in = take(n), take(n)
    nodes_in = take(6)
    outs = take(4)
    dq_out = take(n + 1)
    kbuf, vbuf, kturn, qbuf, wide_in, wide_out, dkv, dq, listed, sems = take(10)
    count = [0]

    def start(src, dst):
        copy = pltpu.make_async_copy(src, dst, sems.at[count[0]])
        count[0] += 1
        copy.start()
        return copy

    copies = []
    for dx in range(4):
        for core in range(2):
            piece = nodes_in[4 + dx // 2].at[pl.ds(dx % 2 * 256, 256)] if core else nodes_in[dx]
            for dy in range(4):
                rows = pl.ds((dx * 2 + dy % 2) * BLOCK + (core * 2 + dy // 2) * SHARD, SHARD)
                copies.append(start(piece.at[pl.ds(dy * 64, SHARD)], kbuf.at[rows]))
                copies.append(start(piece.at[pl.ds(dy * 64 + SHARD, SHARD)], vbuf.at[rows]))
    for i in range(n):
        copies.append(start(q_in[i], qbuf.at[pl.ds(i * PACKED, BLOCK)]))
        copies.append(start(g_in[i], qbuf.at[pl.ds(i * PACKED + BLOCK, BLOCK + AUX)]))
    dq[...] = jnp.zeros_like(dq)
    wide_in[...] = jnp.zeros_like(wide_in)
    wide_out[...] = jnp.zeros_like(wide_out)
    dkv[...] = jnp.zeros_like(dkv)
    for copy in copies:
        copy.wait()
    for h in range(HEADS):
        for j in range(8):
            block = kbuf[pl.ds(j * BLOCK, BLOCK), pl.ds(h * HD, HD)]
            kturn[j, pl.ds(h * HD, HD), :] = block.T

    def pair(i, ja, jb, dead):
        rows_a = pl.ds(pl.multiple_of(ja * BLOCK, BLOCK), BLOCK)
        rows_b = pl.ds(pl.multiple_of(jb * BLOCK, BLOCK), BLOCK)
        aux_rows = pl.ds(pl.multiple_of(i * PACKED + 2 * BLOCK, AUX), AUX)
        second = lax.broadcasted_iota(jnp.int32, (2 * BLOCK, 1), 0) >= BLOCK
        shut = jnp.where(second, dead, 0.0)

        def first_dot(h):
            cols = pl.ds(h * HD, HD)
            k = jnp.concatenate([kbuf[rows_a, cols], kbuf[rows_b, cols]], axis=0)
            v = jnp.concatenate([vbuf[rows_a, cols], vbuf[rows_b, cols]], axis=0)
            return jnp.dot(
                jnp.concatenate([k, v], axis=1), wide_in[h], preferred_element_type=jnp.float32
            )

        def middle(h, both):
            cols = pl.ds(h * HD, HD)
            aux = qbuf[aux_rows, cols].astype(jnp.float32)
            lse = (aux[0:1] + aux[1:2] + aux[2:3]) * LOG2E
            delta = aux[3:4] + aux[4:5] + aux[5:6]
            weights = jnp.exp2(both[:, :HD] * (SCALE * LOG2E) - (lse + shut))
            scores_low = (weights * (both[:, HD:] - delta)).astype(jnp.bfloat16)
            return weights.astype(jnp.bfloat16), scores_low

        def node_dot(h, lows):
            wide = pl.ds(h * 2 * HD, 2 * HD)
            part = jnp.dot(
                jnp.concatenate(lows, axis=1), wide_out[h], preferred_element_type=jnp.float32
            )
            dkv[rows_a, wide] += part[:BLOCK]
            dkv[rows_b, wide] += part[BLOCK:]

        def query_dot(h, low):
            cols = pl.ds(h * HD, HD)
            k_turned = jnp.concatenate([kturn[ja, cols, :], kturn[jb, cols, :]], axis=1)
            dq[pl.ds(pl.multiple_of(i * D, D) + h * HD, HD), :] += jnp.dot(
                k_turned, low, preferred_element_type=jnp.float32
            )

        def query_dots(h, even_low, low):
            two = pl.ds(h * HD, 2 * HD)
            turned = jnp.dot(
                jnp.concatenate([kturn[ja, two, :], kturn[jb, two, :]], axis=1),
                jnp.concatenate([even_low, low], axis=1),
                preferred_element_type=jnp.float32,
            )
            at = pl.multiple_of(i * D, D) + h * HD
            dq[pl.ds(at, HD), :] += turned[:HD, :HD]
            dq[pl.ds(at + HD, HD), :] += turned[HD:, HD:]


        lows = [middle(h, first_dot(h)) for h in range(HEADS)]
        for h in range(HEADS):
            node_dot(h, lows[h])
        for h in range(0, HEADS, 2):
            query_dots(h, lows[h][1], lows[h + 1][1])

    @pl.loop(0, n)
    def _(i):
        total = jnp.int32(0)
        last_one = jnp.int32(0)
        for j in range(8):
            here = mask_ref[i * 8 + j]
            listed[total] = j
            last_one = jnp.where(here != 0, j, last_one)
            total = total + here
        listed[total] = last_one

        @pl.when(total > 0)
        def _():
            rows = pl.ds(pl.multiple_of(i * PACKED, AUX), BLOCK)
            grad_rows = pl.ds(pl.multiple_of(i * PACKED + BLOCK, AUX), BLOCK)
            for h in range(HEADS):
                cols = pl.ds(h * HD, HD)
                q, g = qbuf[rows, cols], qbuf[grad_rows, cols]
                wide_in[h, pl.ds(0, HD), pl.ds(0, HD)] = q.T
                wide_in[h, pl.ds(HD, HD), pl.ds(HD, HD)] = g.T
                wide_out[h, pl.ds(0, HD), pl.ds(0, HD)] = g
                wide_out[h, pl.ds(HD, HD), pl.ds(HD, HD)] = q

            @pl.loop(0, (total + 1) // 2)
            def _(p):
                alone = 2 * p + 1 >= total
                dead = jnp.where(alone, jnp.float32(1e30), jnp.float32(0.0))
                pair(i, listed[2 * p], listed[2 * p + 1], dead)

    for i in range(n):
        for h in range(HEADS):
            cols = pl.ds(h * HD, HD)
            turned = (dq[pl.ds(i * D + h * HD, HD), :] * SCALE).astype(jnp.bfloat16).T
            if i == n - 1:
                dq_out[i][:, cols] = turned[:64]
                dq_out[i + 1][:, cols] = turned[64:]
            else:
                dq_out[i][:, cols] = turned
    for core in range(2):
        for dx in range(4):
            for dy in range(4):
                rows = pl.ds((dx * 2 + dy % 2) * BLOCK + (core * 2 + dy // 2) * SHARD, SHARD)
                k_to = pl.ds((dx * 4 + dy) * SHARD, SHARD)
                v_to = pl.ds((dy * 4 + dx) * SHARD, SHARD)
                for h in range(HEADS):
                    cols = pl.ds(h * HD, HD)
                    part = dkv[rows, pl.ds(h * 2 * HD, HD)]
                    outs[2 + core][v_to, cols] = part.astype(jnp.bfloat16)
                    part = dkv[rows, pl.ds(h * 2 * HD + HD, HD)] * SCALE
                    outs[core][k_to, cols] = part.astype(jnp.bfloat16)


def tiles(mask, q_blocks, g_blocks, nodes):
    n = len(q_blocks)
    bf16, f32 = jnp.bfloat16, jnp.float32
    scratch = [
        pltpu.VMEM((1024, D), bf16),
        pltpu.VMEM((1024, D), bf16),
        pltpu.VMEM((8, 1024, BLOCK), bf16),
        pltpu.VMEM((n * PACKED, D), bf16),
        pltpu.VMEM((HEADS, 2 * HD, 2 * HD), bf16),
        pltpu.VMEM((HEADS, 2 * HD, 2 * HD), bf16),
        pltpu.VMEM((1024, 2 * D), f32),
        pltpu.VMEM((n * D, BLOCK), f32),
        pltpu.SMEM((16,), jnp.int32),
        pltpu.SemaphoreType.DMA((64 + 2 * n,)),
    ]
    sums = [jax.ShapeDtypeStruct((512, D), bf16)] * 4
    blocks = [jax.ShapeDtypeStruct((BLOCK, D), bf16)] * (n - 1)
    blocks += [jax.ShapeDtypeStruct((64, D), bf16)] * 2
    args = list(q_blocks) + list(g_blocks) + list(nodes)
    out = pl.pallas_call(
        functools.partial(tile_kernel, n),
        out_shape=sums + blocks,
        in_specs=[pl.BlockSpec(memory_space=pltpu.SMEM)]
        + [pl.BlockSpec(memory_space=pltpu.HBM)] * len(args),
        out_specs=[pl.BlockSpec(memory_space=pltpu.VMEM)] * (len(sums) + len(blocks)),
        scratch_shapes=scratch,
        compiler_params=pltpu.CompilerParams(vmem_limit_bytes=40 * 2**20),
        cost_estimate=pl.CostEstimate(
            flops=20_000_000_000, bytes_accessed=12_000_000, transcendentals=0
        ),
    )(mask, *args)
    return list(out[:4]), list(out[4:])


def fence_kernel(*refs):
    pass


def fence(*arrays, space=pltpu.HBM):
    any_space = pl.BlockSpec(memory_space=space)
    return pl.pallas_call(
        fence_kernel,
        out_shape=[jax.ShapeDtypeStruct(a.shape, a.dtype) for a in arrays],
        in_specs=[any_space] * len(arrays),
        out_specs=[any_space] * len(arrays),
        input_output_aliases={at: at for at in range(len(arrays))},
        compiler_params=pltpu.CompilerParams(vmem_limit_bytes=2**20),
        cost_estimate=pl.CostEstimate(flops=10_000_000_000, bytes_accessed=4096, transcendentals=0),
    )(*arrays)


def plain_call(kernel, out_shapes, *arrays):
    return pl.pallas_call(
        kernel,
        out_shape=[jax.ShapeDtypeStruct(shape, jnp.bfloat16) for shape in out_shapes],
        compiler_params=pltpu.CompilerParams(vmem_limit_bytes=16 * 2**20),
        cost_estimate=pl.CostEstimate(flops=5_000_000_000, bytes_accessed=4_000_000, transcendentals=0),
    )(*arrays)


def wide_sum(*parts):
    total = parts[0].astype(jnp.float32)
    for part in parts[1:]:
        total = total + part.astype(jnp.float32)
    return total.astype(jnp.bfloat16)


def sum_kernel_1(far_a, far_b, up, down, k_own, k_got, v_own, v_got, up_out, down_out, *pieces):
    low, high = pl.ds(0, 64), pl.ds(64, 64)
    up_out[low, :] = wide_sum(far_a[...], up[low, :])
    up_out[high, :] = up[high, :]
    down_out[low, :] = down[low, :]
    down_out[high, :] = wide_sum(far_b[...], down[high, :])
    for d in range(4):
        rows = pl.ds(d * BLOCK, BLOCK)
        pieces[d][...] = wide_sum(k_own[rows, :], k_got[rows, :])
        pieces[4 + d][...] = wide_sum(v_own[rows, :], v_got[rows, :])


def hop_kernel(up_got, up, down_got, down, token, up_out, down_out, token_out):
    up_out[...] = wide_sum(up_got[...], up[...])
    down_out[...] = wide_sum(down_got[...], down[...])
    token_out[...] = token[...]


def node_kernel_1(*refs):
    k_parts, v_parts, outs = refs[:4], refs[4:8], refs[9:]
    for d in range(4):
        rows = pl.ds(d * SHARD, SHARD)
        outs[d][...] = wide_sum(*[part[rows, :] for part in k_parts])
        outs[4 + d][...] = wide_sum(*[part[rows, :] for part in v_parts])


def node_kernel_2(*refs):
    refs[8][...] = wide_sum(*[part[...] for part in refs[:4]])
    refs[9][...] = wide_sum(*[part[...] for part in refs[4:8]])


def home_kernel(own, up_got, down_got, token, out, token_out):
    out[...] = wide_sum(own[...], up_got[...], down_got[...])
    token_out[...] = token[...]


def local(query, d_out, out, lse, keys, values, tile_blocks, tile_count):
    row, col = lax.axis_index("qrow"), lax.axis_index("ncol")
    x, core, z, yl = row // 4, row % 2, col // 2, col % 2
    home = z_home(0)
    up, down = z_step(1), z_step(-1)
    whole, shard = (BLOCK, D), (SHARD, D)

    token = jnp.zeros((8, 128), jnp.float32)
    cell = jnp.concatenate(
        [tile_blocks.reshape(64), tile_count.reshape(1), jnp.zeros((63,), jnp.int32)]
    ).reshape(1, 128)
    q, g = {0: send(query, home)}, {}
    group = (0, 1, -1, 2, -2, 3, -3, 4)
    kv = jnp.concatenate([keys, values], axis=0)
    packed = pack(d_out, out, lse)
    token, q[0], kv, cell, packed = fence(token, q[0], kv, cell, packed)
    q[-1], q[1] = send(q[0], up), send(q[0], down)
    g[0] = send(packed, home)
    kv_y = [kv] + [send(kv, y_step(-d)) for d in (1, 3, 2)]
    kv_y = jnp.concatenate([kv_y[0], kv_y[1], kv_y[3], kv_y[2]], axis=0)
    token, g[0], kv_y = fence(token, g[0], kv_y)
    kv_x = {1: send(kv_y, x_step(-1))}
    g[-1], g[1] = send(g[0], up), send(g[0], down)
    token, q[-1], q[1] = fence(token, q[-1], q[1])
    q[-2], q[2] = send(q[-1], up), send(q[1], down)
    token, g[-1], g[1], kv_x[1], kv_y = fence(token, g[-1], g[1], kv_x[1], kv_y)
    g[-2], g[2] = send(g[-1], up), send(g[1], down)
    kv_x[3] = send(kv_y, x_step(-3))
    token, q[-2], q[2] = fence(token, q[-2], q[2])
    q[-3], q[3] = send(q[-2], up), send(q[2], down)
    token, g[-2], g[2], kv_x[3], kv_y = fence(token, g[-2], g[2], kv_x[3], kv_y)
    g[-3], g[3] = send(g[-2], up), send(g[2], down)
    kv_x[2] = send(kv_y, x_step(-2))
    kv_x[0] = kv_y
    cells = [(send(cell, home), core), (send(cell, OTHER_CELL), 1 - core)]
    mask = jnp.zeros((64,), jnp.bool_)
    for got, column in cells:
        a, b, count = got[0, 0:32], got[0, 32:64], got[0, 64]
        alive = (jnp.arange(32) < count) & ((a & 1) == core)
        slot = (((a >> 1) - z) & 7) * 8 + ((b - x) & 3) * 2 + (column ^ yl)
        hits = alive[:, None] & (slot[:, None] == jnp.arange(64)[None, :])
        mask = mask | jnp.any(hits, axis=0)
    mask = mask.astype(jnp.int32).reshape(8, 8)[jnp.array([o % 8 for o in group])].reshape(64)

    token, q[-3], q[3] = fence(token, q[-3], q[3])
    q[4] = send(q[-3], up)
    low_pieces = jnp.concatenate([kv_x[0], kv_x[1]], axis=0)
    token, g[-3], g[3], q[4], kv_x[2], low_pieces, mask = fence(
        token, g[-3], g[3], q[4], kv_x[2], low_pieces, mask
    )
    g[4] = send(g[3], down)
    low_got = send(low_pieces, CORE)
    high_got = send(jnp.concatenate([kv_x[2], kv_x[3]], axis=0), CORE)
    nodes = [kv_x[0], kv_x[1], kv_x[2], kv_x[3], low_got, high_got]

    sums, parts = tiles(mask, [q[o] for o in group], [g[o] for o in group], nodes)
    dq = dict(zip(group, parts))
    k_own, k_oth, v_own, v_oth = sums

    k_got, v_got = send(k_oth, CORE), send(v_oth, CORE)
    own = send(dq[0], home)
    held = plain_call(
        sum_kernel_1, [whole] * 10,
        send(parts[7], up), send(parts[8], down), dq[3], dq[-3], k_own, k_got, v_own, v_got,
    )
    up_low, down_low = held[0], held[1]
    k_low, v_low = list(held[2:6]), list(held[6:10])
    k_parts, v_parts = [k_low[0]] + [None] * 3, [v_low[0]] + [None] * 3
    k_parts[1] = send(k_low[1], x_step(1))
    v_parts[1], v_parts[3] = send(v_low[1], y_step(1)), send(v_low[3], y_step(3))
    token = jnp.zeros((16, 128), jnp.bfloat16)
    hop_shapes = [whole, whole, token.shape]
    up_low, down_low, token = plain_call(
        hop_kernel, hop_shapes, send(up_low, up), dq[2], send(down_low, down), dq[-2], token
    )
    up_got, down_got = send(up_low, up), send(down_low, down)
    token, own, k_parts[1], v_parts[1], v_parts[3], k_low[2], k_low[3], v_low[2] = fence(
        token, own, k_parts[1], v_parts[1], v_parts[3], k_low[2], k_low[3], v_low[2],
        space=pl.ANY,
    )
    k_parts[3], k_parts[2] = send(k_low[3], x_step(3)), send(k_low[2], x_step(2))
    v_parts[2] = send(v_low[2], y_step(2))
    up_low, down_low, token = plain_call(
        hop_kernel, hop_shapes, up_got, dq[1], down_got, dq[-1], token
    )
    up_got, down_got = send(up_low, z_home(1)), send(down_low, z_home(-1))
    grad_query, token = plain_call(home_kernel, [whole, token.shape], own, up_got, down_got, token)
    held = plain_call(node_kernel_1, [shard] * 8, *k_parts, *v_parts, token)
    k_parts = [held[0]] + [send(held[d], y_step(d)) for d in (1, 2, 3)]
    v_parts = [held[4]] + [send(held[4 + d], x_step(d)) for d in (1, 2, 3)]
    grad_keys, grad_values = plain_call(node_kernel_2, [shard] * 2, *k_parts, *v_parts)
    return grad_query, grad_keys, grad_values


def solution(mesh):
    in_specs = (
        P(("qrow", "ncol"), None),
        P(("qrow", "ncol"), None),
        P(("qrow", "ncol"), None),
        P(None, ("qrow", "ncol")),
        P(("ncol", "qrow"), None),
        P(("ncol", "qrow"), None),
        P("qrow", "ncol", None, None),
        P("qrow", "ncol"),
    )
    out_specs = (P(("qrow", "ncol"), None), P(("ncol", "qrow"), None), P(("ncol", "qrow"), None))
    return jax.shard_map(local, mesh=mesh, in_specs=in_specs, out_specs=out_specs, check_vma=False)
```

```python
import functools

import jax
import jax.numpy as jnp
from jax import lax
from jax.experimental import pallas as pl
from jax.experimental.pallas import tpu as pltpu
from jax.sharding import PartitionSpec as P


BLOCK = 128
HEADS = 8
HD = 128
D = 1024
SHARD = 32
AUX = 16
PACKED = 2 * BLOCK + AUX
AXES = ("qrow", "ncol")
SCALE = HD ** (-0.5)
LOG2E = 1.4426950408889634


def device_index(x, yh, core, z, yl):
    return (x * 4 + yh * 2 + core) * 16 + z * 2 + yl


def make_perm(target):
    pairs = []
    for x in range(4):
        for yh in range(2):
            for core in range(2):
                for z in range(8):
                    for yl in range(2):
                        pairs.append(
                            (
                                device_index(x, yh, core, z, yl),
                                device_index(*target(x, yh, core, z, yl)),
                            )
                        )
    return pairs


def y_step(d):
    def target(x, yh, core, z, yl):
        y = (yh * 2 + yl + d) % 4
        return (x, y // 2, core, z, y % 2)

    return make_perm(target)


def x_step(d):
    return make_perm(lambda x, yh, core, z, yl: ((x + d) % 4, yh, core, z, yl))


def z_step(d):
    return make_perm(lambda x, yh, core, z, yl: (x, yh, core, (z + d) % 8, yl))


def z_home(d):
    return make_perm(lambda x, yh, core, z, yl: (x, yh, yl, (z + d) % 8, core))


CORE = make_perm(lambda x, yh, core, z, yl: (x, yh, 1 - core, z, yl))
OTHER_CELL = make_perm(lambda x, yh, core, z, yl: (x, yh, 1 - yl, z, core))


def send(array, perm):
    return lax.ppermute(array, AXES, perm)


def split3(value):
    high = value.astype(jnp.bfloat16).astype(jnp.float32)
    rest = value - high
    middle = rest.astype(jnp.bfloat16).astype(jnp.float32)
    return high, middle, rest - middle


def pack_kernel(grad_ref, out_ref, lse_ref, packed_ref):
    packed_ref[pl.ds(0, BLOCK), :] = grad_ref[...]
    row = lax.broadcasted_iota(jnp.int32, (AUX, BLOCK), 0)
    for h in range(HEADS):
        cols = pl.ds(h * HD, HD)
        product = grad_ref[:, cols].astype(jnp.float32) * out_ref[:, cols].astype(jnp.float32)
        delta = jnp.sum(product.T, axis=0, keepdims=True)
        parts = split3(lse_ref[pl.ds(h, 1), :]) + split3(delta)
        aux = jnp.zeros((AUX, BLOCK), jnp.float32)
        for at, part in enumerate(parts):
            aux = jnp.where(row == at, jnp.broadcast_to(part, (AUX, BLOCK)), aux)
        packed_ref[pl.ds(BLOCK, AUX), cols] = aux.astype(jnp.bfloat16)


def pack(d_out, out, lse):
    return pl.pallas_call(
        pack_kernel,
        out_shape=jax.ShapeDtypeStruct((BLOCK + AUX, D), jnp.bfloat16),
        compiler_params=pltpu.CompilerParams(vmem_limit_bytes=16 * 2**20),
        cost_estimate=pl.CostEstimate(flops=20_000_000_000, bytes_accessed=800_000, transcendentals=0),
    )(d_out, out, lse)


def tile_kernel(n, mask_ref, *refs):
    refs = list(refs)

    def take(count):
        got = refs[:count]
        del refs[:count]
        return got

    q_in, g_in = take(n), take(n)
    nodes_in = take(6)
    outs = take(4)
    dq_out = take(n + 1)
    kbuf, vbuf, kturn, qbuf, wide_in, wide_out, dkv, dq, listed, sems = take(10)
    count = [0]

    def start(src, dst):
        copy = pltpu.make_async_copy(src, dst, sems.at[count[0]])
        count[0] += 1
        copy.start()
        return copy

    copies = []
    for dx in range(4):
        for core in range(2):
            piece = nodes_in[4 + dx // 2].at[pl.ds(dx % 2 * 256, 256)] if core else nodes_in[dx]
            for dy in range(4):
                rows = pl.ds((dx * 2 + dy % 2) * BLOCK + (core * 2 + dy // 2) * SHARD, SHARD)
                copies.append(start(piece.at[pl.ds(dy * 64, SHARD)], kbuf.at[rows]))
                copies.append(start(piece.at[pl.ds(dy * 64 + SHARD, SHARD)], vbuf.at[rows]))
    for i in range(n):
        copies.append(start(q_in[i], qbuf.at[pl.ds(i * PACKED, BLOCK)]))
        copies.append(start(g_in[i], qbuf.at[pl.ds(i * PACKED + BLOCK, BLOCK + AUX)]))
    dq[...] = jnp.zeros_like(dq)
    wide_in[...] = jnp.zeros_like(wide_in)
    wide_out[...] = jnp.zeros_like(wide_out)
    dkv[...] = jnp.zeros_like(dkv)
    for copy in copies[:64]:
        copy.wait()
    for h in range(HEADS):
        for j in range(8):
            block = kbuf[pl.ds(j * BLOCK, BLOCK), pl.ds(h * HD, HD)]
            kturn[j, pl.ds(h * HD, HD), :] = block.T
    for copy in copies[64:]:
        copy.wait()

    def pair(i, ja, jb, dead):
        rows_a = pl.ds(pl.multiple_of(ja * BLOCK, BLOCK), BLOCK)
        rows_b = pl.ds(pl.multiple_of(jb * BLOCK, BLOCK), BLOCK)
        aux_rows = pl.ds(pl.multiple_of(i * PACKED + 2 * BLOCK, AUX), AUX)
        second = lax.broadcasted_iota(jnp.int32, (2 * BLOCK, 1), 0) >= BLOCK
        shut = jnp.where(second, dead, 0.0)

        def first_dot(h):
            cols = pl.ds(h * HD, HD)
            k = jnp.concatenate([kbuf[rows_a, cols], kbuf[rows_b, cols]], axis=0)
            v = jnp.concatenate([vbuf[rows_a, cols], vbuf[rows_b, cols]], axis=0)
            return jnp.dot(
                jnp.concatenate([k, v], axis=1), wide_in[h], preferred_element_type=jnp.float32
            )

        def middle(h, both):
            cols = pl.ds(h * HD, HD)
            aux = qbuf[aux_rows, cols].astype(jnp.float32)
            lse = (aux[0:1] + aux[1:2] + aux[2:3]) * LOG2E
            delta = aux[3:4] + aux[4:5] + aux[5:6]
            weights = jnp.exp2(both[:, :HD] * (SCALE * LOG2E) - (lse + shut))
            scores_low = (weights * (both[:, HD:] - delta)).astype(jnp.bfloat16)
            return weights.astype(jnp.bfloat16), scores_low

        def node_dot(h, lows):
            wide = pl.ds(h * 2 * HD, 2 * HD)
            part = jnp.dot(
                jnp.concatenate(lows, axis=1), wide_out[h], preferred_element_type=jnp.float32
            )
            dkv[rows_a, wide] += part[:BLOCK]
            dkv[rows_b, wide] += part[BLOCK:]

        def query_dot(h, low):
            cols = pl.ds(h * HD, HD)
            k_turned = jnp.concatenate([kturn[ja, cols, :], kturn[jb, cols, :]], axis=1)
            dq[pl.ds(pl.multiple_of(i * D, D) + h * HD, HD), :] += jnp.dot(
                k_turned, low, preferred_element_type=jnp.float32
            )

        def query_dots(h, even_low, low):
            two = pl.ds(h * HD, 2 * HD)
            turned = jnp.dot(
                jnp.concatenate([kturn[ja, two, :], kturn[jb, two, :]], axis=1),
                jnp.concatenate([even_low, low], axis=1),
                preferred_element_type=jnp.float32,
            )
            at = pl.multiple_of(i * D, D) + h * HD
            dq[pl.ds(at, HD), :] += turned[:HD, :HD]
            dq[pl.ds(at + HD, HD), :] += turned[HD:, HD:]


        lows = [middle(h, first_dot(h)) for h in range(HEADS)]
        for h in range(HEADS):
            node_dot(h, lows[h])
        for h in range(0, HEADS, 2):
            query_dots(h, lows[h][1], lows[h + 1][1])

    @pl.loop(0, n)
    def _(i):
        total = jnp.int32(0)
        last_one = jnp.int32(0)
        for j in range(8):
            here = mask_ref[i * 8 + j]
            listed[total] = j
            last_one = jnp.where(here != 0, j, last_one)
            total = total + here
        listed[total] = last_one

        @pl.when(total > 0)
        def _():
            rows = pl.ds(pl.multiple_of(i * PACKED, AUX), BLOCK)
            grad_rows = pl.ds(pl.multiple_of(i * PACKED + BLOCK, AUX), BLOCK)
            for h in range(HEADS):
                cols = pl.ds(h * HD, HD)
                q, g = qbuf[rows, cols], qbuf[grad_rows, cols]
                wide_in[h, pl.ds(0, HD), pl.ds(0, HD)] = q.T
                wide_in[h, pl.ds(HD, HD), pl.ds(HD, HD)] = g.T
                wide_out[h, pl.ds(0, HD), pl.ds(0, HD)] = g
                wide_out[h, pl.ds(HD, HD), pl.ds(HD, HD)] = q

            @pl.loop(0, (total + 1) // 2)
            def _(p):
                alone = 2 * p + 1 >= total
                dead = jnp.where(alone, jnp.float32(1e30), jnp.float32(0.0))
                pair(i, listed[2 * p], listed[2 * p + 1], dead)

    for i in range(n):
        for h in range(HEADS):
            cols = pl.ds(h * HD, HD)
            turned = (dq[pl.ds(i * D + h * HD, HD), :] * SCALE).astype(jnp.bfloat16).T
            if i == n - 1:
                dq_out[i][:, cols] = turned[:64]
                dq_out[i + 1][:, cols] = turned[64:]
            else:
                dq_out[i][:, cols] = turned
    for core in range(2):
        for dx in range(4):
            for dy in range(4):
                rows = pl.ds((dx * 2 + dy % 2) * BLOCK + (core * 2 + dy // 2) * SHARD, SHARD)
                k_to = pl.ds((dx * 4 + dy) * SHARD, SHARD)
                v_to = pl.ds((dy * 4 + dx) * SHARD, SHARD)
                for h in range(HEADS):
                    cols = pl.ds(h * HD, HD)
                    part = dkv[rows, pl.ds(h * 2 * HD, HD)]
                    outs[2 + core][v_to, cols] = part.astype(jnp.bfloat16)
                    part = dkv[rows, pl.ds(h * 2 * HD + HD, HD)] * SCALE
                    outs[core][k_to, cols] = part.astype(jnp.bfloat16)


def tiles(mask, q_blocks, g_blocks, nodes):
    n = len(q_blocks)
    bf16, f32 = jnp.bfloat16, jnp.float32
    scratch = [
        pltpu.VMEM((1024, D), bf16),
        pltpu.VMEM((1024, D), bf16),
        pltpu.VMEM((8, 1024, BLOCK), bf16),
        pltpu.VMEM((n * PACKED, D), bf16),
        pltpu.VMEM((HEADS, 2 * HD, 2 * HD), bf16),
        pltpu.VMEM((HEADS, 2 * HD, 2 * HD), bf16),
        pltpu.VMEM((1024, 2 * D), f32),
        pltpu.VMEM((n * D, BLOCK), f32),
        pltpu.SMEM((16,), jnp.int32),
        pltpu.SemaphoreType.DMA((64 + 2 * n,)),
    ]
    sums = [jax.ShapeDtypeStruct((512, D), bf16)] * 4
    blocks = [jax.ShapeDtypeStruct((BLOCK, D), bf16)] * (n - 1)
    blocks += [jax.ShapeDtypeStruct((64, D), bf16)] * 2
    args = list(q_blocks) + list(g_blocks) + list(nodes)
    out = pl.pallas_call(
        functools.partial(tile_kernel, n),
        out_shape=sums + blocks,
        in_specs=[pl.BlockSpec(memory_space=pltpu.SMEM)]
        + [pl.BlockSpec(memory_space=pltpu.HBM)] * len(args),
        out_specs=[pl.BlockSpec(memory_space=pltpu.VMEM)] * (len(sums) + len(blocks)),
        scratch_shapes=scratch,
        compiler_params=pltpu.CompilerParams(vmem_limit_bytes=40 * 2**20),
        cost_estimate=pl.CostEstimate(
            flops=20_000_000_000, bytes_accessed=12_000_000, transcendentals=0
        ),
    )(mask, *args)
    return list(out[:4]), list(out[4:])


def fence_kernel(*refs):
    pass


def fence(*arrays, space=pltpu.HBM):
    any_space = pl.BlockSpec(memory_space=space)
    return pl.pallas_call(
        fence_kernel,
        out_shape=[jax.ShapeDtypeStruct(a.shape, a.dtype) for a in arrays],
        in_specs=[any_space] * len(arrays),
        out_specs=[any_space] * len(arrays),
        input_output_aliases={at: at for at in range(len(arrays))},
        compiler_params=pltpu.CompilerParams(vmem_limit_bytes=2**20),
        cost_estimate=pl.CostEstimate(flops=10_000_000_000, bytes_accessed=4096, transcendentals=0),
    )(*arrays)


def plain_call(kernel, out_shapes, *arrays):
    return pl.pallas_call(
        kernel,
        out_shape=[jax.ShapeDtypeStruct(shape, jnp.bfloat16) for shape in out_shapes],
        compiler_params=pltpu.CompilerParams(vmem_limit_bytes=16 * 2**20),
        cost_estimate=pl.CostEstimate(flops=5_000_000_000, bytes_accessed=4_000_000, transcendentals=0),
    )(*arrays)


def wide_sum(*parts):
    total = parts[0].astype(jnp.float32)
    for part in parts[1:]:
        total = total + part.astype(jnp.float32)
    return total.astype(jnp.bfloat16)


def sum_kernel_1(far_a, far_b, up, down, k_own, k_got, v_own, v_got, up_out, down_out, *pieces):
    low, high = pl.ds(0, 64), pl.ds(64, 64)
    up_out[low, :] = wide_sum(far_a[...], up[low, :])
    up_out[high, :] = up[high, :]
    down_out[low, :] = down[low, :]
    down_out[high, :] = wide_sum(far_b[...], down[high, :])
    for d in range(4):
        rows = pl.ds(d * BLOCK, BLOCK)
        pieces[d][...] = wide_sum(k_own[rows, :], k_got[rows, :])
        pieces[4 + d][...] = wide_sum(v_own[rows, :], v_got[rows, :])


def hop_kernel(up_got, up, down_got, down, token, up_out, down_out, token_out):
    up_out[...] = wide_sum(up_got[...], up[...])
    down_out[...] = wide_sum(down_got[...], down[...])
    token_out[...] = token[...]


def node_kernel_1(*refs):
    k_parts, v_parts, outs = refs[:4], refs[4:8], refs[9:]
    for d in range(4):
        rows = pl.ds(d * SHARD, SHARD)
        outs[d][...] = wide_sum(*[part[rows, :] for part in k_parts])
        outs[4 + d][...] = wide_sum(*[part[rows, :] for part in v_parts])


def node_kernel_2(*refs):
    refs[8][...] = wide_sum(*[part[...] for part in refs[:4]])
    refs[9][...] = wide_sum(*[part[...] for part in refs[4:8]])


def home_kernel(own, up_got, down_got, token, out, token_out):
    out[...] = wide_sum(own[...], up_got[...], down_got[...])
    token_out[...] = token[...]


def local(query, d_out, out, lse, keys, values, tile_blocks, tile_count):
    row, col = lax.axis_index("qrow"), lax.axis_index("ncol")
    x, core, z, yl = row // 4, row % 2, col // 2, col % 2
    home = z_home(0)
    up, down = z_step(1), z_step(-1)
    whole, shard = (BLOCK, D), (SHARD, D)

    token = jnp.zeros((8, 128), jnp.float32)
    cell = jnp.concatenate(
        [tile_blocks.reshape(64), tile_count.reshape(1), jnp.zeros((63,), jnp.int32)]
    ).reshape(1, 128)
    q, g = {0: send(query, home)}, {}
    group = (0, 1, -1, 2, -2, 3, -3, 4)
    kv = jnp.concatenate([keys, values], axis=0)
    packed = pack(d_out, out, lse)
    token, q[0], kv, cell, packed = fence(token, q[0], kv, cell, packed)
    q[-1], q[1] = send(q[0], up), send(q[0], down)
    g[0] = send(packed, home)
    kv_y = [kv] + [send(kv, y_step(-d)) for d in (1, 3, 2)]
    kv_y = jnp.concatenate([kv_y[0], kv_y[1], kv_y[3], kv_y[2]], axis=0)
    token, g[0], kv_y = fence(token, g[0], kv_y)
    kv_x = {1: send(kv_y, x_step(-1))}
    g[-1], g[1] = send(g[0], up), send(g[0], down)
    token, q[-1], q[1] = fence(token, q[-1], q[1])
    q[-2], q[2] = send(q[-1], up), send(q[1], down)
    token, g[-1], g[1], kv_x[1], kv_y = fence(token, g[-1], g[1], kv_x[1], kv_y)
    g[-2], g[2] = send(g[-1], up), send(g[1], down)
    kv_x[3] = send(kv_y, x_step(-3))
    token, q[-2], q[2] = fence(token, q[-2], q[2])
    q[-3], q[3] = send(q[-2], up), send(q[2], down)
    token, g[-2], g[2], kv_x[3], kv_y = fence(token, g[-2], g[2], kv_x[3], kv_y)
    g[-3], g[3] = send(g[-2], up), send(g[2], down)
    kv_x[2] = send(kv_y, x_step(-2))
    kv_x[0] = kv_y
    cells = [(send(cell, home), core), (send(cell, OTHER_CELL), 1 - core)]
    mask = jnp.zeros((64,), jnp.bool_)
    for got, column in cells:
        a, b, count = got[0, 0:32], got[0, 32:64], got[0, 64]
        alive = (jnp.arange(32) < count) & ((a & 1) == core)
        slot = (((a >> 1) - z) & 7) * 8 + ((b - x) & 3) * 2 + (column ^ yl)
        hits = alive[:, None] & (slot[:, None] == jnp.arange(64)[None, :])
        mask = mask | jnp.any(hits, axis=0)
    mask = mask.astype(jnp.int32).reshape(8, 8)[jnp.array([o % 8 for o in group])].reshape(64)

    token, q[-3], q[3] = fence(token, q[-3], q[3])
    q[4] = send(q[-3], up)
    low_pieces = jnp.concatenate([kv_x[0], kv_x[1]], axis=0)
    token, g[-3], g[3], q[4], kv_x[2], low_pieces, mask = fence(
        token, g[-3], g[3], q[4], kv_x[2], low_pieces, mask
    )
    g[4] = send(g[3], down)
    low_got = send(low_pieces, CORE)
    high_got = send(jnp.concatenate([kv_x[2], kv_x[3]], axis=0), CORE)
    nodes = [kv_x[0], kv_x[1], kv_x[2], kv_x[3], low_got, high_got]

    sums, parts = tiles(mask, [q[o] for o in group], [g[o] for o in group], nodes)
    dq = dict(zip(group, parts))
    k_own, k_oth, v_own, v_oth = sums

    k_got, v_got = send(k_oth, CORE), send(v_oth, CORE)
    own = send(dq[0], home)
    held = plain_call(
        sum_kernel_1, [whole] * 10,
        send(parts[7], up), send(parts[8], down), dq[3], dq[-3], k_own, k_got, v_own, v_got,
    )
    up_low, down_low = held[0], held[1]
    k_low, v_low = list(held[2:6]), list(held[6:10])
    k_parts, v_parts = [k_low[0]] + [None] * 3, [v_low[0]] + [None] * 3
    k_parts[1] = send(k_low[1], x_step(1))
    v_parts[1], v_parts[3] = send(v_low[1], y_step(1)), send(v_low[3], y_step(3))
    token = jnp.zeros((16, 128), jnp.bfloat16)
    hop_shapes = [whole, whole, token.shape]
    up_low, down_low, token = plain_call(
        hop_kernel, hop_shapes, send(up_low, up), dq[2], send(down_low, down), dq[-2], token
    )
    up_got, down_got = send(up_low, up), send(down_low, down)
    token, own, k_parts[1], v_parts[1], v_parts[3], k_low[2], k_low[3], v_low[2] = fence(
        token, own, k_parts[1], v_parts[1], v_parts[3], k_low[2], k_low[3], v_low[2],
        space=pl.ANY,
    )
    k_parts[3], k_parts[2] = send(k_low[3], x_step(3)), send(k_low[2], x_step(2))
    v_parts[2] = send(v_low[2], y_step(2))
    up_low, down_low, token = plain_call(
        hop_kernel, hop_shapes, up_got, dq[1], down_got, dq[-1], token
    )
    up_got, down_got = send(up_low, z_home(1)), send(down_low, z_home(-1))
    grad_query, token = plain_call(home_kernel, [whole, token.shape], own, up_got, down_got, token)
    held = plain_call(node_kernel_1, [shard] * 8, *k_parts, *v_parts, token)
    k_parts = [held[0]] + [send(held[d], y_step(d)) for d in (1, 2, 3)]
    v_parts = [held[4]] + [send(held[4 + d], x_step(d)) for d in (1, 2, 3)]
    grad_keys, grad_values = plain_call(node_kernel_2, [shard] * 2, *k_parts, *v_parts)
    return grad_query, grad_keys, grad_values


def solution(mesh):
    in_specs = (
        P(("qrow", "ncol"), None),
        P(("qrow", "ncol"), None),
        P(("qrow", "ncol"), None),
        P(None, ("qrow", "ncol")),
        P(("ncol", "qrow"), None),
        P(("ncol", "qrow"), None),
        P("qrow", "ncol", None, None),
        P("qrow", "ncol"),
    )
    out_specs = (P(("qrow", "ncol"), None), P(("ncol", "qrow"), None), P(("ncol", "qrow"), None))
    return jax.shard_map(local, mesh=mesh, in_specs=in_specs, out_specs=out_specs, check_vma=False)
```

```python
import functools

import jax
import jax.numpy as jnp
from jax import lax
from jax.experimental import pallas as pl
from jax.experimental.pallas import tpu as pltpu
from jax.sharding import PartitionSpec as P


BLOCK = 128
HEADS = 8
HD = 128
D = 1024
SHARD = 32
AUX = 16
PACKED = 2 * BLOCK + AUX
AXES = ("qrow", "ncol")
SCALE = HD ** (-0.5)
LOG2E = 1.4426950408889634


def device_index(x, yh, core, z, yl):
    return (x * 4 + yh * 2 + core) * 16 + z * 2 + yl


def make_perm(target):
    pairs = []
    for x in range(4):
        for yh in range(2):
            for core in range(2):
                for z in range(8):
                    for yl in range(2):
                        pairs.append(
                            (
                                device_index(x, yh, core, z, yl),
                                device_index(*target(x, yh, core, z, yl)),
                            )
                        )
    return pairs


def y_step(d):
    def target(x, yh, core, z, yl):
        y = (yh * 2 + yl + d) % 4
        return (x, y // 2, core, z, y % 2)

    return make_perm(target)


def x_step(d):
    return make_perm(lambda x, yh, core, z, yl: ((x + d) % 4, yh, core, z, yl))


def z_step(d):
    return make_perm(lambda x, yh, core, z, yl: (x, yh, core, (z + d) % 8, yl))


def z_home(d):
    return make_perm(lambda x, yh, core, z, yl: (x, yh, yl, (z + d) % 8, core))


CORE = make_perm(lambda x, yh, core, z, yl: (x, yh, 1 - core, z, yl))
OTHER_CELL = make_perm(lambda x, yh, core, z, yl: (x, yh, 1 - yl, z, core))


def send(array, perm):
    return lax.ppermute(array, AXES, perm)


def split3(value):
    high = value.astype(jnp.bfloat16).astype(jnp.float32)
    rest = value - high
    middle = rest.astype(jnp.bfloat16).astype(jnp.float32)
    return high, middle, rest - middle


def pack_kernel(grad_ref, out_ref, lse_ref, packed_ref):
    packed_ref[pl.ds(0, BLOCK), :] = grad_ref[...]
    row = lax.broadcasted_iota(jnp.int32, (AUX, BLOCK), 0)
    for h in range(HEADS):
        cols = pl.ds(h * HD, HD)
        product = grad_ref[:, cols].astype(jnp.float32) * out_ref[:, cols].astype(jnp.float32)
        delta = jnp.sum(product.T, axis=0, keepdims=True)
        parts = split3(lse_ref[pl.ds(h, 1), :]) + split3(delta)
        aux = jnp.zeros((AUX, BLOCK), jnp.float32)
        for at, part in enumerate(parts):
            aux = jnp.where(row == at, jnp.broadcast_to(part, (AUX, BLOCK)), aux)
        packed_ref[pl.ds(BLOCK, AUX), cols] = aux.astype(jnp.bfloat16)


def pack(d_out, out, lse):
    return pl.pallas_call(
        pack_kernel,
        out_shape=jax.ShapeDtypeStruct((BLOCK + AUX, D), jnp.bfloat16),
        compiler_params=pltpu.CompilerParams(vmem_limit_bytes=16 * 2**20),
        cost_estimate=pl.CostEstimate(flops=20_000_000_000, bytes_accessed=800_000, transcendentals=0),
    )(d_out, out, lse)


def tile_kernel(n, mask_ref, *refs):
    refs = list(refs)

    def take(count):
        got = refs[:count]
        del refs[:count]
        return got

    q_in, g_in = take(n), take(n)
    nodes_in = take(6)
    outs = take(4)
    dq_out = take(n + 1)
    kbuf, vbuf, kturn, qbuf, wide_in, wide_out, dkv, dq, listed, sems = take(10)
    count = [0]

    def start(src, dst):
        copy = pltpu.make_async_copy(src, dst, sems.at[count[0]])
        count[0] += 1
        copy.start()
        return copy

    copies = []
    for dx in range(4):
        for core in range(2):
            if core == 0:
                piece = nodes_in[dx]
            elif dx == 2:
                piece = nodes_in[5]
            else:
                piece = nodes_in[4].at[pl.ds(min(dx, 2) * 256, 256)]
            for dy in range(4):
                rows = pl.ds((dx * 2 + dy % 2) * BLOCK + (core * 2 + dy // 2) * SHARD, SHARD)
                copies.append(start(piece.at[pl.ds(dy * 64, SHARD)], kbuf.at[rows]))
                copies.append(start(piece.at[pl.ds(dy * 64 + SHARD, SHARD)], vbuf.at[rows]))
    for i in range(n):
        copies.append(start(q_in[i], qbuf.at[pl.ds(i * PACKED, BLOCK)]))
        copies.append(start(g_in[i], qbuf.at[pl.ds(i * PACKED + BLOCK, BLOCK + AUX)]))
    dq[...] = jnp.zeros_like(dq)
    wide_in[...] = jnp.zeros_like(wide_in)
    wide_out[...] = jnp.zeros_like(wide_out)
    dkv[...] = jnp.zeros_like(dkv)
    for copy in copies:
        copy.wait()
    for h in range(HEADS):
        for j in range(8):
            block = kbuf[pl.ds(j * BLOCK, BLOCK), pl.ds(h * HD, HD)]
            kturn[j, pl.ds(h * HD, HD), :] = block.T

    def pair(i, ja, jb, dead):
        rows_a = pl.ds(pl.multiple_of(ja * BLOCK, BLOCK), BLOCK)
        rows_b = pl.ds(pl.multiple_of(jb * BLOCK, BLOCK), BLOCK)
        aux_rows = pl.ds(pl.multiple_of(i * PACKED + 2 * BLOCK, AUX), AUX)
        second = lax.broadcasted_iota(jnp.int32, (2 * BLOCK, 1), 0) >= BLOCK
        shut = jnp.where(second, dead, 0.0)

        def first_dot(h):
            cols = pl.ds(h * HD, HD)
            k = jnp.concatenate([kbuf[rows_a, cols], kbuf[rows_b, cols]], axis=0)
            v = jnp.concatenate([vbuf[rows_a, cols], vbuf[rows_b, cols]], axis=0)
            return jnp.dot(
                jnp.concatenate([k, v], axis=1), wide_in[h], preferred_element_type=jnp.float32
            )

        def middle(h, both):
            cols = pl.ds(h * HD, HD)
            aux = qbuf[aux_rows, cols].astype(jnp.float32)
            lse = (aux[0:1] + aux[1:2] + aux[2:3]) * LOG2E
            delta = aux[3:4] + aux[4:5] + aux[5:6]
            weights = jnp.exp2(both[:, :HD] * (SCALE * LOG2E) - (lse + shut))
            scores_low = (weights * (both[:, HD:] - delta)).astype(jnp.bfloat16)
            return weights.astype(jnp.bfloat16), scores_low

        def node_dot(h, lows):
            wide = pl.ds(h * 2 * HD, 2 * HD)
            part = jnp.dot(
                jnp.concatenate(lows, axis=1), wide_out[h], preferred_element_type=jnp.float32
            )
            dkv[rows_a, wide] += part[:BLOCK]
            dkv[rows_b, wide] += part[BLOCK:]

        def query_dot(h, low):
            cols = pl.ds(h * HD, HD)
            k_turned = jnp.concatenate([kturn[ja, cols, :], kturn[jb, cols, :]], axis=1)
            dq[pl.ds(pl.multiple_of(i * D, D) + h * HD, HD), :] += jnp.dot(
                k_turned, low, preferred_element_type=jnp.float32
            )

        def query_dots(h, even_low, low):
            two = pl.ds(h * HD, 2 * HD)
            turned = jnp.dot(
                jnp.concatenate([kturn[ja, two, :], kturn[jb, two, :]], axis=1),
                jnp.concatenate([even_low, low], axis=1),
                preferred_element_type=jnp.float32,
            )
            at = pl.multiple_of(i * D, D) + h * HD
            dq[pl.ds(at, HD), :] += turned[:HD, :HD]
            dq[pl.ds(at + HD, HD), :] += turned[HD:, HD:]


        lows = [middle(h, first_dot(h)) for h in range(HEADS)]
        for h in range(HEADS):
            node_dot(h, lows[h])
        for h in range(0, HEADS, 2):
            query_dots(h, lows[h][1], lows[h + 1][1])

    @pl.loop(0, n)
    def _(i):
        total = jnp.int32(0)
        last_one = jnp.int32(0)
        for j in range(8):
            here = mask_ref[i * 8 + j]
            listed[total] = j
            last_one = jnp.where(here != 0, j, last_one)
            total = total + here
        listed[total] = last_one

        @pl.when(total > 0)
        def _():
            rows = pl.ds(pl.multiple_of(i * PACKED, AUX), BLOCK)
            grad_rows = pl.ds(pl.multiple_of(i * PACKED + BLOCK, AUX), BLOCK)
            for h in range(HEADS):
                cols = pl.ds(h * HD, HD)
                q, g = qbuf[rows, cols], qbuf[grad_rows, cols]
                wide_in[h, pl.ds(0, HD), pl.ds(0, HD)] = q.T
                wide_in[h, pl.ds(HD, HD), pl.ds(HD, HD)] = g.T
                wide_out[h, pl.ds(0, HD), pl.ds(0, HD)] = g
                wide_out[h, pl.ds(HD, HD), pl.ds(HD, HD)] = q

            @pl.loop(0, (total + 1) // 2)
            def _(p):
                alone = 2 * p + 1 >= total
                dead = jnp.where(alone, jnp.float32(1e30), jnp.float32(0.0))
                pair(i, listed[2 * p], listed[2 * p + 1], dead)

    for i in range(n):
        for h in range(HEADS):
            cols = pl.ds(h * HD, HD)
            turned = (dq[pl.ds(i * D + h * HD, HD), :] * SCALE).astype(jnp.bfloat16).T
            if i == n - 1:
                dq_out[i][:, cols] = turned[:64]
                dq_out[i + 1][:, cols] = turned[64:]
            else:
                dq_out[i][:, cols] = turned
    for core in range(2):
        for dx in range(4):
            for dy in range(4):
                rows = pl.ds((dx * 2 + dy % 2) * BLOCK + (core * 2 + dy // 2) * SHARD, SHARD)
                k_to = pl.ds((dx * 4 + dy) * SHARD, SHARD)
                v_to = pl.ds((dy * 4 + dx) * SHARD, SHARD)
                for h in range(HEADS):
                    cols = pl.ds(h * HD, HD)
                    part = dkv[rows, pl.ds(h * 2 * HD, HD)]
                    outs[2 + core][v_to, cols] = part.astype(jnp.bfloat16)
                    part = dkv[rows, pl.ds(h * 2 * HD + HD, HD)] * SCALE
                    outs[core][k_to, cols] = part.astype(jnp.bfloat16)


def tiles(mask, q_blocks, g_blocks, nodes):
    n = len(q_blocks)
    bf16, f32 = jnp.bfloat16, jnp.float32
    scratch = [
        pltpu.VMEM((1024, D), bf16),
        pltpu.VMEM((1024, D), bf16),
        pltpu.VMEM((8, 1024, BLOCK), bf16),
        pltpu.VMEM((n * PACKED, D), bf16),
        pltpu.VMEM((HEADS, 2 * HD, 2 * HD), bf16),
        pltpu.VMEM((HEADS, 2 * HD, 2 * HD), bf16),
        pltpu.VMEM((1024, 2 * D), f32),
        pltpu.VMEM((n * D, BLOCK), f32),
        pltpu.SMEM((16,), jnp.int32),
        pltpu.SemaphoreType.DMA((64 + 2 * n,)),
    ]
    sums = [jax.ShapeDtypeStruct((512, D), bf16)] * 4
    blocks = [jax.ShapeDtypeStruct((BLOCK, D), bf16)] * (n - 1)
    blocks += [jax.ShapeDtypeStruct((64, D), bf16)] * 2
    args = list(q_blocks) + list(g_blocks) + list(nodes)
    out = pl.pallas_call(
        functools.partial(tile_kernel, n),
        out_shape=sums + blocks,
        in_specs=[pl.BlockSpec(memory_space=pltpu.SMEM)]
        + [pl.BlockSpec(memory_space=pltpu.HBM)] * len(args),
        out_specs=[pl.BlockSpec(memory_space=pltpu.VMEM)] * (len(sums) + len(blocks)),
        scratch_shapes=scratch,
        compiler_params=pltpu.CompilerParams(vmem_limit_bytes=40 * 2**20),
        cost_estimate=pl.CostEstimate(
            flops=20_000_000_000, bytes_accessed=12_000_000, transcendentals=0
        ),
    )(mask, *args)
    return list(out[:4]), list(out[4:])


def fence_kernel(*refs):
    pass


def fence(*arrays, space=pltpu.HBM):
    any_space = pl.BlockSpec(memory_space=space)
    return pl.pallas_call(
        fence_kernel,
        out_shape=[jax.ShapeDtypeStruct(a.shape, a.dtype) for a in arrays],
        in_specs=[any_space] * len(arrays),
        out_specs=[any_space] * len(arrays),
        input_output_aliases={at: at for at in range(len(arrays))},
        compiler_params=pltpu.CompilerParams(vmem_limit_bytes=2**20),
        cost_estimate=pl.CostEstimate(flops=10_000_000_000, bytes_accessed=4096, transcendentals=0),
    )(*arrays)


def plain_call(kernel, out_shapes, *arrays):
    return pl.pallas_call(
        kernel,
        out_shape=[jax.ShapeDtypeStruct(shape, jnp.bfloat16) for shape in out_shapes],
        compiler_params=pltpu.CompilerParams(vmem_limit_bytes=16 * 2**20),
        cost_estimate=pl.CostEstimate(flops=5_000_000_000, bytes_accessed=4_000_000, transcendentals=0),
    )(*arrays)


def wide_sum(*parts):
    total = parts[0].astype(jnp.float32)
    for part in parts[1:]:
        total = total + part.astype(jnp.float32)
    return total.astype(jnp.bfloat16)


def sum_kernel_1(far_a, far_b, up, down, k_own, k_got, v_own, v_got, up_out, down_out, *pieces):
    low, high = pl.ds(0, 64), pl.ds(64, 64)
    up_out[low, :] = wide_sum(far_a[...], up[low, :])
    up_out[high, :] = up[high, :]
    down_out[low, :] = down[low, :]
    down_out[high, :] = wide_sum(far_b[...], down[high, :])
    for d in range(4):
        rows = pl.ds(d * BLOCK, BLOCK)
        pieces[d][...] = wide_sum(k_own[rows, :], k_got[rows, :])
        pieces[4 + d][...] = wide_sum(v_own[rows, :], v_got[rows, :])


def hop_kernel(up_got, up, down_got, down, token, up_out, down_out, token_out):
    up_out[...] = wide_sum(up_got[...], up[...])
    down_out[...] = wide_sum(down_got[...], down[...])
    token_out[...] = token[...]


def node_kernel_1(*refs):
    k_parts, v_parts, outs = refs[:4], refs[4:8], refs[9:]
    for d in range(4):
        rows = pl.ds(d * SHARD, SHARD)
        outs[d][...] = wide_sum(*[part[rows, :] for part in k_parts])
        outs[4 + d][...] = wide_sum(*[part[rows, :] for part in v_parts])


def node_kernel_2(*refs):
    refs[8][...] = wide_sum(*[part[...] for part in refs[:4]])
    refs[9][...] = wide_sum(*[part[...] for part in refs[4:8]])


def home_kernel(own, up_got, down_got, token, out, token_out):
    out[...] = wide_sum(own[...], up_got[...], down_got[...])
    token_out[...] = token[...]


def local(query, d_out, out, lse, keys, values, tile_blocks, tile_count):
    row, col = lax.axis_index("qrow"), lax.axis_index("ncol")
    x, core, z, yl = row // 4, row % 2, col // 2, col % 2
    home = z_home(0)
    up, down = z_step(1), z_step(-1)
    whole, shard = (BLOCK, D), (SHARD, D)

    token = jnp.zeros((8, 128), jnp.float32)
    cell = jnp.concatenate(
        [tile_blocks.reshape(64), tile_count.reshape(1), jnp.zeros((63,), jnp.int32)]
    ).reshape(1, 128)
    q, g = {0: send(query, home)}, {}
    group = (0, 1, -1, 2, -2, 3, -3, 4)
    kv = jnp.concatenate([keys, values], axis=0)
    packed = pack(d_out, out, lse)
    token, q[0], kv, cell, packed = fence(token, q[0], kv, cell, packed)
    q[-1], q[1] = send(q[0], up), send(q[0], down)
    g[0] = send(packed, home)
    kv_y = [kv] + [send(kv, y_step(-d)) for d in (1, 3, 2)]
    kv_y = jnp.concatenate([kv_y[0], kv_y[1], kv_y[3], kv_y[2]], axis=0)
    token, g[0], kv_y = fence(token, g[0], kv_y)
    kv_x = {1: send(kv_y, x_step(-1))}
    g[-1], g[1] = send(g[0], up), send(g[0], down)
    token, q[-1], q[1] = fence(token, q[-1], q[1])
    q[-2], q[2] = send(q[-1], up), send(q[1], down)
    token, g[-1], g[1], kv_x[1], kv_y = fence(token, g[-1], g[1], kv_x[1], kv_y)
    g[-2], g[2] = send(g[-1], up), send(g[1], down)
    kv_x[3] = send(kv_y, x_step(-3))
    token, q[-2], q[2] = fence(token, q[-2], q[2])
    q[-3], q[3] = send(q[-2], up), send(q[2], down)
    token, g[-2], g[2], kv_x[3], kv_y = fence(token, g[-2], g[2], kv_x[3], kv_y)
    g[-3], g[3] = send(g[-2], up), send(g[2], down)
    kv_x[2] = send(kv_y, x_step(-2))
    kv_x[0] = kv_y
    cells = [(send(cell, home), core), (send(cell, OTHER_CELL), 1 - core)]
    mask = jnp.zeros((64,), jnp.bool_)
    for got, column in cells:
        a, b, count = got[0, 0:32], got[0, 32:64], got[0, 64]
        alive = (jnp.arange(32) < count) & ((a & 1) == core)
        slot = (((a >> 1) - z) & 7) * 8 + ((b - x) & 3) * 2 + (column ^ yl)
        hits = alive[:, None] & (slot[:, None] == jnp.arange(64)[None, :])
        mask = mask | jnp.any(hits, axis=0)
    mask = mask.astype(jnp.int32).reshape(8, 8)[jnp.array([o % 8 for o in group])].reshape(64)

    token, q[-3], q[3] = fence(token, q[-3], q[3])
    q[4] = send(q[-3], up)
    low_pieces = jnp.concatenate([kv_x[0], kv_x[1], kv_x[3]], axis=0)
    token, g[-3], g[3], q[4], kv_x[2], low_pieces, mask = fence(
        token, g[-3], g[3], q[4], kv_x[2], low_pieces, mask
    )
    g[4] = send(g[3], down)
    low_got = send(low_pieces, CORE)
    high_got = send(kv_x[2], CORE)
    nodes = [kv_x[0], kv_x[1], kv_x[2], kv_x[3], low_got, high_got]

    sums, parts = tiles(mask, [q[o] for o in group], [g[o] for o in group], nodes)
    dq = dict(zip(group, parts))
    k_own, k_oth, v_own, v_oth = sums

    k_got, v_got = send(k_oth, CORE), send(v_oth, CORE)
    own = send(dq[0], home)
    held = plain_call(
        sum_kernel_1, [whole] * 10,
        send(parts[7], up), send(parts[8], down), dq[3], dq[-3], k_own, k_got, v_own, v_got,
    )
    up_low, down_low = held[0], held[1]
    k_low, v_low = list(held[2:6]), list(held[6:10])
    k_parts, v_parts = [k_low[0]] + [None] * 3, [v_low[0]] + [None] * 3
    k_parts[1] = send(k_low[1], x_step(1))
    v_parts[1], v_parts[3] = send(v_low[1], y_step(1)), send(v_low[3], y_step(3))
    token = jnp.zeros((16, 128), jnp.bfloat16)
    hop_shapes = [whole, whole, token.shape]
    up_low, down_low, token = plain_call(
        hop_kernel, hop_shapes, send(up_low, up), dq[2], send(down_low, down), dq[-2], token
    )
    up_got, down_got = send(up_low, up), send(down_low, down)
    token, own, k_parts[1], v_parts[1], v_parts[3], k_low[2], k_low[3], v_low[2] = fence(
        token, own, k_parts[1], v_parts[1], v_parts[3], k_low[2], k_low[3], v_low[2],
        space=pl.ANY,
    )
    k_parts[3], k_parts[2] = send(k_low[3], x_step(3)), send(k_low[2], x_step(2))
    v_parts[2] = send(v_low[2], y_step(2))
    up_low, down_low, token = plain_call(
        hop_kernel, hop_shapes, up_got, dq[1], down_got, dq[-1], token
    )
    up_got, down_got = send(up_low, z_home(1)), send(down_low, z_home(-1))
    grad_query, token = plain_call(home_kernel, [whole, token.shape], own, up_got, down_got, token)
    held = plain_call(node_kernel_1, [shard] * 8, *k_parts, *v_parts, token)
    k_parts = [held[0]] + [send(held[d], y_step(d)) for d in (1, 2, 3)]
    v_parts = [held[4]] + [send(held[4 + d], x_step(d)) for d in (1, 2, 3)]
    grad_keys, grad_values = plain_call(node_kernel_2, [shard] * 2, *k_parts, *v_parts)
    return grad_query, grad_keys, grad_values


def solution(mesh):
    in_specs = (
        P(("qrow", "ncol"), None),
        P(("qrow", "ncol"), None),
        P(("qrow", "ncol"), None),
        P(None, ("qrow", "ncol")),
        P(("ncol", "qrow"), None),
        P(("ncol", "qrow"), None),
        P("qrow", "ncol", None, None),
        P("qrow", "ncol"),
    )
    out_specs = (P(("qrow", "ncol"), None), P(("ncol", "qrow"), None), P(("ncol", "qrow"), None))
    return jax.shard_map(local, mesh=mesh, in_specs=in_specs, out_specs=out_specs, check_vma=False)
```
